128 devices in a mesh: gx: 8 (over z, x_hi), gy: 4 (over x_lo, core), gz: 4 (over y).
Axes of the slice: x: 4 (x_hi: 2, x_lo: 2; x = x_hi * 2 + x_lo), y: 4, z: 4, core: 2. Of those that a mesh axis runs over, the one named last changes fastest.
Arguments:
- layer_input: bfloat16 [4, 1024, 16384], P('gy', 'gz', 'gx'), may hold values from -6 to 6
- qkv_grad: bfloat16 [4, 1024, 9216], P('gy', 'gx', 'gz'), may hold values from -0.25 to 0.25
- qkv_weight: bfloat16 [16384, 9216], P(('gx', 'gy'), 'gz'), may hold values from -6 to 6
Outputs:
- input_grad: bfloat16 [4, 1024, 16384], P('gy', None, ('gx', 'gz'))
- weight_grad: bfloat16 [16384, 9216], P(('gx', 'gy'), 'gz')
The draws below stay inside these ranges and needn't reach their ends.
All inputs are finite; a program needn't handle non-finite values.
Results may differ from the reference program's by a relative error of at most 0.015.
Values may be sent and summed in bfloat16 or wider, within the bound.
A program may use at most 128 MiB of HBM per device.

```python
import jax
import jax.numpy as jnp
from jax import lax

D = 16384
GROUP_ROWS = 1024
NQKV = 9216
GROUPS = 4
N_GY = 4


def block_scale(stream_key, shape, pieces, low, top_value):
    gain, own = 1.0, jax.random.fold_in(stream_key, 6)
    for axis_at, blocks in pieces:
        draws = jnp.exp(jax.random.uniform(jax.random.fold_in(own, axis_at), (blocks,), jnp.float32, low / len(pieces), top_value / len(pieces)))
        gain = gain * jnp.repeat(draws, shape[axis_at] // blocks).reshape([-1 if axis == axis_at else 1 for axis in range(len(shape))])
    return gain


def centred(stream_key, extent, deviation, bound, split=(), dtype=jnp.bfloat16):
    values = jax.random.normal(stream_key, extent, jnp.float32) * deviation
    if len(split) > 0:
        values = block_scale(stream_key, extent, split, -0.22, 0.18) * values
    return jnp.clip(values, min=-bound, max=bound).astype(dtype)


def setup_inputs(seed: int = 0) -> dict:
    keys = jax.random.split(jax.random.key(seed), 4)
    layer_input = centred(keys[0], (GROUPS, GROUP_ROWS, D), 1.0, 6.0, ((0, 4), (1, 4), (2, 8)))
    qkv_grad = centred(keys[1], (GROUPS, GROUP_ROWS, NQKV), ((GROUP_ROWS * N_GY) ** -0.5), 0.25, ((0, 4), (1, 8), (2, 4)))
    qkv_weight = centred(keys[2], (D, NQKV), ((GROUP_ROWS * N_GY) ** 0.5 * NQKV ** -0.5), 6.0, ((0, 32), (1, 4)))
    return {"layer_input": layer_input, "qkv_grad": qkv_grad, "qkv_weight": qkv_weight}


def reference(layer_input, qkv_grad, qkv_weight):
    flat_grad = qkv_grad.reshape(GROUPS * GROUP_ROWS, NQKV)
    input_grad = jnp.dot(flat_grad, qkv_weight.T, preferred_element_type=jnp.float32)
    input_grad = input_grad.astype(jnp.bfloat16).reshape(GROUPS, GROUP_ROWS, D)
    summed = jnp.zeros((D, NQKV), jnp.float32)
    for index in range(GROUPS):
        partial_term = jnp.dot(layer_input[index].T, qkv_grad[index], preferred_element_type=jnp.float32)
        rounded = lax.optimization_barrier(partial_term.astype(jnp.bfloat16))
        summed = summed + rounded.astype(jnp.float32)
    return input_grad, summed.astype(jnp.bfloat16)
```

```python
import jax
import jax.numpy as jnp
from jax import lax
from jax.experimental import pallas as pl
from jax.experimental.pallas import tpu as pltpu
from jax.sharding import PartitionSpec as P

MESH = pl.DeviceIdType.MESH
BF = jnp.bfloat16
F32 = jnp.float32
N = 2304
NMSG = 96


def m4(v):
    return lax.rem(v + 8, 4)


def swap12(v):
    return lax.div(v, 2) + 2 * lax.rem(v, 2)


def kernel(x_in, g_in, w_in, dx_out, dw_out, G, X, W, PB, RS, ACC, DWB, ssem, rsem, lsem, dsem):
    gx, gy, gz = lax.axis_index("gx"), lax.axis_index("gy"), lax.axis_index("gz")
    x_hi, z = lax.rem(gx, 2), lax.div(gx, 2)
    x_lo, c = lax.div(gy, 2), lax.rem(gy, 2)
    x, y, k = x_hi * 2 + x_lo, gz, gy
    oc = 1 - c
    xpair = x + 1 - 2 * x_lo

    def dev(dx=0, dy=0, dz=0):
        xx = m4(x + dx)
        return (m4(z + dz) * 2 + lax.div(xx, 2), lax.rem(xx, 2) * 2 + c, m4(y + dy))

    XP, XM, YP, YM, ZP, ZM = dev(dx=1), dev(dx=-1), dev(dy=1), dev(dy=-1), dev(dz=1), dev(dz=-1)
    SIB = (gx, x_lo * 2 + oc, y)
    PAIR = (gx, (1 - x_lo) * 2 + c, y)
    PAIRO = (gx, (1 - x_lo) * 2 + oc, y)
    is_self = jnp.logical_and(k == 0, y == 0)
    not_self = jnp.logical_not(is_self)
    TDST = (gx, swap12(m4(y - k)), k)
    TSRC = (gx, y, m4(y + swap12(k)))

    sends = []

    def send(src, dst, device):
        i = len(sends)
        copy = pltpu.make_async_remote_copy(
            src_ref=src,
            dst_ref=dst,
            send_sem=ssem.at[i],
            recv_sem=rsem.at[i],
            device_id=device,
            device_id_type=MESH,
        )
        sends.append(copy)
        copy.start()
        return copy

    def got(*copies):
        for copy in copies:
            copy.wait_recv()

    def shard(dz, dx, lo=0, rows=128, core=None):
        xx = m4(x + dx)
        slot = lax.rem(xx, 2) * 2 + lax.div(xx, 2)
        return G.at[m4(z + dz), c if core is None else core, slot, pl.ds(lo, rows)]

    def xcols(kk):
        return x_in.at[0, :, pl.ds(pl.multiple_of(kk * 512, 512), 512)]

    gs, gs_sib, gs_pair, gs_pairo = c * 2 + x_lo, oc * 2 + x_lo, c * 2 + 1 - x_lo, oc * 2 + 1 - x_lo

    def xslot(dy, g):
        return X.at[m4(y + dy), g]

    own_g = pltpu.make_async_copy(g_in.at[0], shard(0, 0), lsem.at[0])
    own_g.start()
    own_x = pltpu.make_async_copy(xcols(k), xslot(0, gs), lsem.at[1])
    own_x.start()
    own_w = pltpu.make_async_copy(w_in, W, lsem.at[2])
    own_w.start()

    barrier = pltpu.get_barrier_semaphore()
    for device in (XP, XM, YP, YM, ZP, ZM, SIB, PAIRO):
        pl.semaphore_signal(barrier, inc=1, device_id=device, device_id_type=MESH)

    @pl.when(not_self)
    def _():
        pl.semaphore_signal(barrier, inc=1, device_id=TDST, device_id_type=MESH)
        pl.semaphore_signal(barrier, inc=1, device_id=TSRC, device_id_type=MESH)

    pl.semaphore_wait(barrier, jnp.where(is_self, 8, 10))

    xa_pair = send(xcols(lax.rem(k + 2, 4)), xslot(0, gs), PAIR)
    xa_pairo = send(xcols(PAIRO[1]), xslot(0, gs), PAIRO)
    xa_sib = send(xcols(SIB[1]), xslot(0, gs), SIB)

    def own(lo, device):
        return send(g_in.at[0, pl.ds(lo, 64)], shard(0, 0, lo, 64), device)

    gxp0, gxm0, gzp0, gzm0 = own(0, XP), own(0, XM), own(0, ZP), own(0, ZM)
    xyp_own, xym_own = send(xcols(k), xslot(0, gs), YP), send(xcols(k), xslot(0, gs), YM)
    gxp1, gxm1, gzp1, gzm1 = own(64, XP), own(64, XM), own(64, ZP), own(64, ZM)

    def both(ref, plus, minus):
        return send(ref, ref, plus), send(ref, ref, minus)

    got(xa_sib)
    xyp_sib, xym_sib = both(xslot(0, gs_sib), YP, YM)

    got(gxp0)
    gxp2 = send(shard(0, -1, 0, 64), shard(0, -1, 0, 64), XP)
    zsp0, zsm0 = both(shard(0, -1, 0, 64), ZP, ZM)
    got(gzp0)
    gzp2 = send(shard(-1, 0, 0, 64), shard(-1, 0, 0, 64), ZP)
    got(gxm0)
    zsp1, zsm1 = both(shard(0, 1, 0, 64), ZP, ZM)
    got(gzm0)
    got(gzm1)
    gzm2 = send(shard(1, 0, 64, 64), shard(1, 0, 64, 64), ZM)
    xsp1, xsm1 = both(shard(1, 0, 64, 64), XP, XM)
    got(gxm1)
    gxm2 = send(shard(0, 1, 64, 64), shard(0, 1, 64, 64), XM)
    got(gzp1)
    xsp0, xsm0 = both(shard(-1, 0, 64, 64), XP, XM)
    got(gxp1)

    got(xa_pair)
    xyp_pair, xym_pair = both(xslot(0, gs_pair), YP, YM)
    got(xyp_own)
    xfp_own = send(xslot(-1, gs), xslot(-1, gs), YP)
    got(xa_pairo)
    xyp_pairo, xym_pairo = both(xslot(0, gs_pairo), YP, YM)
    got(xym_own)

    got(gxp2)
    zsp2, zsm2 = both(shard(0, 2, 0, 64), ZP, ZM)
    got(gzm2)
    xsp2, xsm2 = both(shard(2, 0, 64, 64), XP, XM)
    got(gxm2)
    own_g.wait()

    def to_sibling(dz):
        ref = G.at[m4(z + dz), c]
        return send(ref, ref, SIB)

    sib0 = to_sibling(0)
    own_w.wait()
    own_x.wait()

    def dx_half(r, dz, core):
        rows = G[m4(z + dz), core].reshape(512, N)
        part = lax.dot_general(rows, W[...], (((1,), (1,)), ((), ())), preferred_element_type=F32)
        PB[r, pl.ds(core * 2, 2)] = part.astype(BF).reshape(2, 2, 128, 512)

    def rs_first(r):
        return (
            send(PB.at[r, m4(y - 1 - k), 0], RS.at[r, 0, 0], YP),
            send(PB.at[r, m4(y + 1 - k), 1], RS.at[r, 1, 0], YM),
        )

    def rs_add(r, step):
        for way, land in ((0, m4(y - 2 - step - k)), (1, m4(y + 2 + step - k))):
            total = RS[r, way, step].astype(F32) + PB[r, land, way].astype(F32)
            RS[r, way, step] = total.astype(BF)

    def rs_next(r, step, copies):
        got(*copies)
        rs_add(r, step)
        return (
            send(RS.at[r, 0, step], RS.at[r, 0, step + 1], YP),
            send(RS.at[r, 1, step], RS.at[r, 1, step + 1], YM),
        )

    last = []

    def rs_last(r, dz, copies):
        got(*copies)
        rs_add(r, 2)
        zi = m4(z + dz)
        for way in range(2):
            row = pl.multiple_of(zi * 256 + way * 128, 128)
            dst = dx_out.at[0, pl.ds(row, 128)]
            i = len(sends) + len(last)
            remote = pltpu.make_async_remote_copy(
                src_ref=RS.at[r, way, 2],
                dst_ref=dst,
                send_sem=ssem.at[NMSG - 1 - len(last)],
                recv_sem=rsem.at[NMSG - 1 - len(last)],
                device_id=TDST,
                device_id_type=MESH,
            )
            local = pltpu.make_async_copy(RS.at[r, way, 2], dst, lsem.at[4 + len(last)])
            last.append((remote, local))
            pl.when(not_self)(remote.start)
            pl.when(is_self)(local.start)

    def dw_block(dz, mode, first=0, last_=3):
        zi = m4(z + dz)

        def tile(i, carry):
            cols = pl.ds(pl.multiple_of(i * 768, 768), 768)
            prod = lax.dot_general(
                X[zi].reshape(1024, 512),
                G[zi, :, :, :, cols].reshape(1024, 768),
                (((0,), (0,)), ((), ())),
                preferred_element_type=F32,
            )
            if mode == 0:
                ACC[:, cols] = prod
            elif mode == 1:
                ACC[:, cols] += prod
            else:
                DWB[:, cols] = (ACC[:, cols] + prod).astype(BF)
            return carry

        lax.fori_loop(first, last_, tile, 0)

    got(zsp0)
    ztp0 = send(shard(-1, -1, 0, 64), shard(-1, -1, 0, 64), ZP)
    got(zsm1)
    ztm1 = send(shard(1, 1, 0, 64), shard(1, 1, 0, 64), ZM)
    got(xsp0)
    xtp0 = send(shard(-1, -1, 64, 64), shard(-1, -1, 64, 64), XP)
    got(xsm1)
    xtm1 = send(shard(1, 1, 64, 64), shard(1, 1, 64, 64), XM)
    got(xym_sib)
    xfm_sib = send(xslot(1, gs_sib), xslot(1, gs_sib), YM)
    got(xyp_sib)

    dx_half(0, 0, c)
    got(sib0)
    dx_half(0, 0, oc)
    rs0 = rs_first(0)

    got(xyp_pair)
    xfp_pair = send(xslot(-1, gs_pair), xslot(-1, gs_pair), YP)
    got(xym_pairo)
    xfm_pairo = send(xslot(1, gs_pairo), xslot(1, gs_pairo), YM)

    got(zsp2)
    ztp2 = send(shard(-1, 2, 0, 32), shard(-1, 2, 0, 32), ZP)
    got(zsm2)
    ztm2 = send(shard(1, 2, 32, 32), shard(1, 2, 32, 32), ZM)
    got(xsp2)
    xtp2 = send(shard(2, -1, 64, 32), shard(2, -1, 64, 32), XP)
    got(xsm2)
    xtm2 = send(shard(2, 1, 96, 32), shard(2, 1, 96, 32), XM)

    rs0 = rs_next(0, 0, rs0)

    got(zsp1, xsm0, xtp0)
    sib1 = to_sibling(-1)
    got(zsm0, xsp1, xtm1)
    sib2 = to_sibling(1)
    rs0 = rs_next(0, 1, rs0)

    dx_half(1, -1, c)
    got(sib1)
    dx_half(1, -1, oc)
    rs1 = rs_first(1)
    dx_half(2, 1, c)
    got(sib2)
    dx_half(2, 1, oc)
    rs2 = rs_first(2)
    rs_last(0, 0, rs0)

    got(gzp2, ztp0, ztm1, ztp2, ztm2, xtp2, xtm2)
    sib3 = to_sibling(2)
    rs1 = rs_next(1, 0, rs1)
    dx_half(3, 2, c)
    rs2 = rs_next(2, 0, rs2)
    got(sib3)
    dx_half(3, 2, oc)
    rs3 = rs_first(3)
    rs1 = rs_next(1, 1, rs1)
    got(xym_pair, xyp_pairo, xfp_own, xfm_sib, xfp_pair, xfm_pairo)
    rs2 = rs_next(2, 1, rs2)
    dw_block(0, 0)
    rs3 = rs_next(3, 0, rs3)
    rs_last(1, -1, rs1)
    rs_last(2, 1, rs2)
    dw_block(-1, 1)
    rs3 = rs_next(3, 1, rs3)
    dw_block(1, 1)
    rs_last(3, 2, rs3)
    dw_block(2, 2)

    out = pltpu.make_async_copy(DWB, dw_out, dsem)
    out.start()
    for copy in sends:
        copy.wait_send()
    for remote, local in last:

        @pl.when(not_self)
        def _(remote=remote):
            remote.wait_send()
            remote.wait_recv()

        pl.when(is_self)(local.wait)
    out.wait()


def body(layer_input, qkv_grad, qkv_weight):
    anyspec = pl.BlockSpec(memory_space=pl.ANY)
    return pl.pallas_call(
        kernel,
        out_shape=(
            jax.ShapeDtypeStruct((1, 1024, 512), BF),
            jax.ShapeDtypeStruct((512, N), BF),
        ),
        in_specs=[anyspec] * 3,
        out_specs=(anyspec, anyspec),
        scratch_shapes=[
            pltpu.VMEM((4, 2, 4, 128, N), BF),
            pltpu.VMEM((4, 4, 256, 512), BF),
            pltpu.VMEM((512, N), BF),
            pltpu.VMEM((4, 4, 2, 128, 512), BF),
            pltpu.VMEM((4, 2, 3, 128, 512), BF),
            pltpu.VMEM((512, N), F32),
            pltpu.VMEM((512, N), BF),
            pltpu.SemaphoreType.DMA((NMSG,)),
            pltpu.SemaphoreType.DMA((NMSG,)),
            pltpu.SemaphoreType.DMA((16,)),
            pltpu.SemaphoreType.DMA,
        ],
        compiler_params=pltpu.CompilerParams(
            collective_id=1, has_side_effects=True, vmem_limit_bytes=60 * 2**20
        ),
        cost_estimate=pl.CostEstimate(
            flops=4 * 4096 * 512 * N, bytes_accessed=8 * 2**20, transcendentals=0
        ),
    )(layer_input, qkv_grad, qkv_weight)


def solution(mesh):
    return jax.shard_map(
        body,
        mesh=mesh,
        in_specs=(P("gy", "gz", "gx"), P("gy", "gx", "gz"), P(("gx", "gy"), "gz")),
        out_specs=(P("gy", None, ("gx", "gz")), P(("gx", "gy"), "gz")),
        check_vma=False,
    )
```

```python
import jax
import jax.numpy as jnp
from jax import lax
from jax.experimental import pallas as pl
from jax.experimental.pallas import tpu as pltpu
from jax.sharding import PartitionSpec as P

MESH = pl.DeviceIdType.MESH
BF = jnp.bfloat16
F32 = jnp.float32
N = 2304
NMSG = 96
H0, H1 = 80, 48
H0A, H1A = 32, 32


def m4(v):
    return lax.rem(v + 8, 4)


def swap12(v):
    return lax.div(v, 2) + 2 * lax.rem(v, 2)


def kernel(x_in, g_in, w_in, dx_out, dw_out, G, X, W, PB, RS, ACC, DWB, ssem, rsem, lsem, dsem):
    gx, gy, gz = lax.axis_index("gx"), lax.axis_index("gy"), lax.axis_index("gz")
    x_hi, z = lax.rem(gx, 2), lax.div(gx, 2)
    x_lo, c = lax.div(gy, 2), lax.rem(gy, 2)
    x, y, k = x_hi * 2 + x_lo, gz, gy
    oc = 1 - c

    def dev(dx=0, dy=0, dz=0):
        xx = m4(x + dx)
        return (m4(z + dz) * 2 + lax.div(xx, 2), lax.rem(xx, 2) * 2 + c, m4(y + dy))

    to_p = 1 - 2 * x_lo
    XP, XQ = dev(dx=to_p), dev(dx=-to_p)
    YP, YM, ZP, ZM = dev(dy=1), dev(dy=-1), dev(dz=1), dev(dz=-1)
    SIB = (gx, x_lo * 2 + oc, y)
    PAIRO = (gx, (1 - x_lo) * 2 + oc, y)
    is_self = jnp.logical_and(k == 0, y == 0)
    not_self = jnp.logical_not(is_self)
    TDST = (gx, swap12(m4(y - k)), k)
    TSRC = (gx, y, m4(y + swap12(k)))

    sends = []

    def send(src, dst, device):
        i = len(sends)
        copy = pltpu.make_async_remote_copy(
            src_ref=src,
            dst_ref=dst,
            send_sem=ssem.at[i],
            recv_sem=rsem.at[i],
            device_id=device,
            device_id_type=MESH,
        )
        sends.append(copy)
        copy.start()
        return copy

    def got(*copies):
        for copy in copies:
            copy.wait_recv()

    def shard(dz, dx, lo=0, rows=128, core=None):
        xx = m4(x + dx)
        slot = lax.rem(xx, 2) * 2 + lax.div(xx, 2)
        return G.at[m4(z + dz), c if core is None else core, slot, pl.ds(lo, rows)]

    def xcols(kk):
        return x_in.at[0, :, pl.ds(pl.multiple_of(kk * 512, 512), 512)]

    gs, gs_sib, gs_pair, gs_pairo = c * 2 + x_lo, oc * 2 + x_lo, c * 2 + 1 - x_lo, oc * 2 + 1 - x_lo

    def xslot(dy, g):
        return X.at[m4(y + dy), g]

    own_g = pltpu.make_async_copy(g_in.at[0], shard(0, 0), lsem.at[0])
    own_g.start()
    own_x = pltpu.make_async_copy(xcols(k), xslot(0, gs), lsem.at[1])
    own_x.start()
    own_w = pltpu.make_async_copy(w_in, W, lsem.at[2])
    own_w.start()

    barrier = pltpu.get_barrier_semaphore()
    for device in (XP, XQ, YP, YM, ZP, ZM, SIB, PAIRO):
        pl.semaphore_signal(barrier, inc=1, device_id=device, device_id_type=MESH)

    @pl.when(not_self)
    def _():
        pl.semaphore_signal(barrier, inc=1, device_id=TDST, device_id_type=MESH)
        pl.semaphore_signal(barrier, inc=1, device_id=TSRC, device_id_type=MESH)

    pl.semaphore_wait(barrier, jnp.where(is_self, 8, 10))

    def own(lo, rows, device):
        return send(g_in.at[0, pl.ds(lo, rows)], shard(0, 0, lo, rows), device)

    gp0, gq0, gzp0, gzm0 = own(0, H0, XP), own(0, H0, XQ), own(0, H0, ZP), own(0, H0, ZM)
    xyp_own, xym_own = send(xcols(k), xslot(0, gs), YP), send(xcols(k), xslot(0, gs), YM)
    xa_sib = send(xcols(SIB[1]), xslot(0, gs), SIB)
    xa_pair = send(xcols(XP[1]), xslot(0, gs), XP)
    gq1, gzp1, gzm1 = own(H0, H1, XQ), own(H0, H1, ZP), own(H0, H1, ZM)

    def both(ref, plus, minus):
        return send(ref, ref, plus), send(ref, ref, minus)

    def to_sibling(dz, lo, rows):
        ref = G.at[m4(z + dz), c, :, pl.ds(lo, rows)]
        return send(ref, ref, SIB)

    def on(ref, device):
        return send(ref, ref, device)

    def dx_half(r, dz, core):
        rows = G[m4(z + dz), core].reshape(512, N)
        part = lax.dot_general(rows, W[...], (((1,), (1,)), ((), ())), preferred_element_type=F32)
        PB[r, pl.ds(core * 2, 2)] = part.astype(BF).reshape(2, 2, 128, 512)

    def land(dy):
        return m4(y + dy - k)

    def rs_start(r):
        return (
            send(PB.at[r, land(2), 0], RS.at[r, 0, 0], YP),
            send(PB.at[r, land(2), 1], RS.at[r, 1, 0], YM),
            send(PB.at[r, land(1), 1], RS.at[r, 0, 1], YP),
            send(PB.at[r, land(-1), 0], RS.at[r, 1, 1], YM),
        )

    def rs_mid(r, copies):
        done = []
        for way, dy, device in ((0, 1, YP), (1, -1, YM)):
            got(copies[way])
            total = RS[r, way, 0].astype(F32) + PB[r, land(dy), way].astype(F32)
            RS[r, way, 0] = total.astype(BF)
            done.append(send(RS.at[r, way, 0], RS.at[r, way, 2], device))
        return (copies[2], copies[3], *done)

    last = []

    def rs_end(r, dz, copies):
        got(*copies)
        zi = m4(z + dz)
        for way in range(2):
            total = PB[r, land(0), way].astype(F32) + RS[r, 1 - way, 1].astype(F32)
            RS[r, way, 2] = (total + RS[r, way, 2].astype(F32)).astype(BF)
            row = pl.multiple_of(zi * 256 + way * 128, 128)
            dst = dx_out.at[0, pl.ds(row, 128)]
            remote = pltpu.make_async_remote_copy(
                src_ref=RS.at[r, way, 2],
                dst_ref=dst,
                send_sem=ssem.at[NMSG - 1 - len(last)],
                recv_sem=rsem.at[NMSG - 1 - len(last)],
                device_id=TDST,
                device_id_type=MESH,
            )
            local = pltpu.make_async_copy(RS.at[r, way, 2], dst, lsem.at[4 + len(last)])
            last.append((remote, local))
            pl.when(not_self)(remote.start)
            pl.when(is_self)(local.start)

    def dw_block(dz, mode, first=0, stop=3):
        zi = m4(z + dz)

        def tile(i, carry):
            cols = pl.ds(pl.multiple_of(i * 768, 768), 768)
            prod = lax.dot_general(
                X[zi].reshape(1024, 512),
                G[zi, :, :, :, cols].reshape(1024, 768),
                (((0,), (0,)), ((), ())),
                preferred_element_type=F32,
            )
            if mode == 0:
                ACC[:, cols] = prod
            elif mode == 1:
                ACC[:, cols] += prod
            else:
                DWB[:, cols] = (ACC[:, cols] + prod).astype(BF)
            return carry

        lax.fori_loop(first, stop, tile, 0)

    P_, Q_ = to_p, -to_p
    got(xa_sib)
    xyp_sib, xym_sib = both(xslot(0, gs_sib), YP, YM)
    got(gq0)
    gp1 = own(H0, H1, XP)
    zsp1, zsm1 = both(shard(0, Q_, 0, H0), ZP, ZM)
    got(xyp_own, xym_own)
    xfp_own = on(xslot(-1, gs), YP)
    got(xyp_sib, xym_sib)
    xfm_sib = on(xslot(1, gs_sib), YM)

    got(gp0)
    gf0 = on(shard(0, P_, 0, H0), XQ)
    zsp0, zsm0 = both(shard(0, P_, 0, H0), ZP, ZM)
    xa_pairo = send(xcols(PAIRO[1]), xslot(0, gs), PAIRO)
    got(xa_pair)
    xyp_pair, xym_pair = both(xslot(0, gs_pair), YP, YM)
    got(gp1)
    gf1 = on(shard(0, P_, H0, H1), XQ)
    got(gq1, gzp0, gzm0)

    got(gf0)
    own_g.wait()
    sib0a = to_sibling(0, 0, H0)
    zsp2, zsm2 = both(shard(0, 2, 0, H0), ZP, ZM)
    got(gzp1)
    xsp0, xsq0 = both(shard(-1, 0, H0, H1), XP, XQ)
    got(gzm1)
    xsp1, xsq1 = both(shard(1, 0, H0, H1), XP, XQ)
    got(xa_pairo)
    xyp_pairo, xym_pairo = both(xslot(0, gs_pairo), YP, YM)
    got(xyp_pair, xym_pair)
    xfp_pair = on(xslot(-1, gs_pair), YP)
    got(gf1)
    sib0b = to_sibling(0, H0, H1)

    own_w.wait()
    own_x.wait()
    dx_half(0, 0, c)
    got(zsp0, zsm0, zsp1, zsm1)
    gzp2 = on(shard(-1, 0, 0, H0), ZP)
    gzm2 = on(shard(1, 0, H0, H1), ZM)
    got(sib0a, sib0b)
    dx_half(0, 0, oc)
    rs0 = rs_start(0)

    got(xsp0)
    xt0 = on(shard(-1, P_, H0, H1), XQ)
    got(xsq1)
    xt1 = on(shard(1, Q_, H0, H1), XP)
    got(zsp2, zsm2)
    sib1a, sib2a = to_sibling(-1, 0, H0), to_sibling(1, 0, H0)
    ztp0, ztm1 = on(shard(-1, P_, 0, H0), ZP), on(shard(1, Q_, 0, H0), ZM)
    got(xym_pairo, xyp_pairo)
    xfm_pairo = on(xslot(1, gs_pairo), YM)
    rs0 = rs_mid(0, rs0)
    got(xsq0, xt0)
    sib1b = to_sibling(-1, H0, H1)
    got(xsp1, xt1)
    sib2b = to_sibling(1, H0, H1)
    got(gzm2)
    xsp2, xsq2 = both(shard(2, 0, H0, H1), XP, XQ)
    ztp2, ztm2 = on(shard(-1, 2, 0, H0A), ZP), on(shard(1, 2, H0A, H0 - H0A), ZM)
    dx_half(1, -1, c)
    got(sib1a, sib1b)
    dx_half(1, -1, oc)
    rs1 = rs_start(1)
    dx_half(2, 1, c)
    got(sib2a, sib2b)
    dx_half(2, 1, oc)
    rs2 = rs_start(2)

    got(xsp2)
    xt2a = on(shard(2, P_, H0, H1A), XQ)
    got(xsq2)
    xt2b = on(shard(2, Q_, H0 + H1A, H1 - H1A), XP)
    rs_end(0, 0, rs0)
    rs1 = rs_mid(1, rs1)
    got(gzp2, ztp0, ztm1, ztp2, ztm2)
    sib3a = to_sibling(2, 0, H0)
    got(xfp_own, xfm_sib, xfp_pair, xfm_pairo)
    dw_block(0, 0, 0, 2)
    got(xt2a, xt2b)
    sib3b = to_sibling(2, H0, H1)
    rs2 = rs_mid(2, rs2)
    dx_half(3, 2, c)
    got(sib3a, sib3b)
    dx_half(3, 2, oc)
    rs3 = rs_start(3)
    dw_block(0, 0, 2)
    dw_block(-1, 1, 0, 2)
    rs3 = rs_mid(3, rs3)
    rs_end(1, -1, rs1)
    rs_end(2, 1, rs2)
    dw_block(-1, 1, 2)
    dw_block(1, 1)
    rs_end(3, 2, rs3)
    dw_block(2, 2)

    out = pltpu.make_async_copy(DWB, dw_out, dsem)
    out.start()
    for copy in sends:
        copy.wait_send()
    for remote, local in last:

        @pl.when(not_self)
        def _(remote=remote):
            remote.wait_send()
            remote.wait_recv()

        pl.when(is_self)(local.wait)
    out.wait()


def copy_kernel(a_in, b_in, a_out, b_out, a_buf, b_buf, in_sem, out_sem):
    parts = []
    for i in range(4):
        rows = pl.ds(i * 128, 128)
        parts.append((b_in.at[rows], b_buf.at[rows], b_out.at[rows]))
    for i in range(4):
        rows = pl.ds(i * 256, 256)
        parts.append((a_in.at[0, rows], a_buf.at[rows], a_out.at[0, rows]))
    reads = [pltpu.make_async_copy(p[0], p[1], in_sem.at[i]) for i, p in enumerate(parts)]
    writes = [pltpu.make_async_copy(p[1], p[2], out_sem.at[i]) for i, p in enumerate(parts)]
    for read in reads:
        read.start()
    for read, write in zip(reads, writes):
        read.wait()
        write.start()
    for write in writes:
        write.wait()


def body(layer_input, qkv_grad, qkv_weight):
    anyspec = pl.BlockSpec(memory_space=pl.ANY)
    results = pl.pallas_call(
        kernel,
        out_shape=(
            jax.ShapeDtypeStruct((1, 1024, 512), BF),
            jax.ShapeDtypeStruct((512, N), BF),
        ),
        in_specs=[anyspec] * 3,
        out_specs=(anyspec, anyspec),
        scratch_shapes=[
            pltpu.VMEM((4, 2, 4, 128, N), BF),
            pltpu.VMEM((4, 4, 256, 512), BF),
            pltpu.VMEM((512, N), BF),
            pltpu.VMEM((4, 4, 2, 128, 512), BF),
            pltpu.VMEM((4, 2, 3, 128, 512), BF),
            pltpu.VMEM((512, N), F32),
            pltpu.VMEM((512, N), BF),
            pltpu.SemaphoreType.DMA((NMSG,)),
            pltpu.SemaphoreType.DMA((NMSG,)),
            pltpu.SemaphoreType.DMA((16,)),
            pltpu.SemaphoreType.DMA,
        ],
        compiler_params=pltpu.CompilerParams(
            collective_id=1, has_side_effects=True, vmem_limit_bytes=60 * 2**20
        ),
        cost_estimate=pl.CostEstimate(
            flops=4 * 4096 * 512 * N, bytes_accessed=8 * 2**20, transcendentals=0
        ),
    )(layer_input, qkv_grad, qkv_weight)
    return pl.pallas_call(
        copy_kernel,
        out_shape=tuple(jax.ShapeDtypeStruct(r.shape, BF) for r in results),
        in_specs=[anyspec] * 2,
        out_specs=(anyspec, anyspec),
        scratch_shapes=[
            pltpu.VMEM((1024, 512), BF),
            pltpu.VMEM((512, N), BF),
            pltpu.SemaphoreType.DMA((8,)),
            pltpu.SemaphoreType.DMA((8,)),
        ],
        compiler_params=pltpu.CompilerParams(vmem_limit_bytes=60 * 2**20),
        cost_estimate=pl.CostEstimate(flops=0, bytes_accessed=7 * 2**20, transcendentals=0),
    )(*results)


def solution(mesh):
    return jax.shard_map(
        body,
        mesh=mesh,
        in_specs=(P("gy", "gz", "gx"), P("gy", "gx", "gz"), P(("gx", "gy"), "gz")),
        out_specs=(P("gy", None, ("gx", "gz")), P(("gx", "gy"), "gz")),
        check_vma=False,
    )
```

```python
import jax
import jax.numpy as jnp
from jax import lax
from jax.experimental import pallas as pl
from jax.experimental.pallas import tpu as pltpu
from jax.sharding import PartitionSpec as P

MESH = pl.DeviceIdType.MESH
BF = jnp.bfloat16
F32 = jnp.float32
N = 2304
NMSG = 128
TILE = 2304
H0, H1 = 80, 48
H0A, H1A = 32, 32


def m4(v):
    return lax.rem(v + 8, 4)


def swap12(v):
    return lax.div(v, 2) + 2 * lax.rem(v, 2)


def kernel(x_in, g_in, w_in, dx_out, dw_out, G, X, W, PB0, PB1, RS0, RS1, ACC, DWB, ssem, rsem, lsem, dsem):
    gx, gy, gz = lax.axis_index("gx"), lax.axis_index("gy"), lax.axis_index("gz")
    x_hi, z = lax.rem(gx, 2), lax.div(gx, 2)
    x_lo, c = lax.div(gy, 2), lax.rem(gy, 2)
    x, y, k = x_hi * 2 + x_lo, gz, gy
    oc = 1 - c

    def dev(dx=0, dy=0, dz=0):
        xx = m4(x + dx)
        return (m4(z + dz) * 2 + lax.div(xx, 2), lax.rem(xx, 2) * 2 + c, m4(y + dy))

    to_p = 1 - 2 * x_lo
    XP, XQ = dev(dx=to_p), dev(dx=-to_p)
    YP, YM, ZP, ZM = dev(dy=1), dev(dy=-1), dev(dz=1), dev(dz=-1)
    SIB = (gx, x_lo * 2 + oc, y)
    PAIRO = (gx, (1 - x_lo) * 2 + oc, y)
    is_self = jnp.logical_and(k == 0, y == 0)
    not_self = jnp.logical_not(is_self)
    TDST = (gx, swap12(m4(y - k)), k)
    TSRC = (gx, y, m4(y + swap12(k)))

    sends = []

    def send(src, dst, device):
        i = len(sends)
        copy = pltpu.make_async_remote_copy(
            src_ref=src,
            dst_ref=dst,
            send_sem=ssem.at[i],
            recv_sem=rsem.at[i],
            device_id=device,
            device_id_type=MESH,
        )
        sends.append(copy)
        copy.start()
        return copy

    def got(*copies):
        for copy in copies:
            copy.wait_recv()

    def shard(dz, dx, lo=0, rows=128, core=None):
        xx = m4(x + dx)
        slot = lax.rem(xx, 2) * 2 + lax.div(xx, 2)
        return G.at[m4(z + dz), c if core is None else core, slot, pl.ds(lo, rows)]

    def xcols(kk):
        return x_in.at[0, :, pl.ds(pl.multiple_of(kk * 512, 512), 512)]

    gs, gs_sib, gs_pair, gs_pairo = c * 2 + x_lo, oc * 2 + x_lo, c * 2 + 1 - x_lo, oc * 2 + 1 - x_lo

    def xslot(dy, g):
        return X.at[m4(y + dy), g]

    own_g = pltpu.make_async_copy(g_in.at[0], shard(0, 0), lsem.at[0])
    own_g.start()
    own_x = pltpu.make_async_copy(xcols(k), xslot(0, gs), lsem.at[1])
    own_x.start()
    own_w = pltpu.make_async_copy(w_in, W, lsem.at[2])
    own_w.start()

    barrier = pltpu.get_barrier_semaphore()
    for device in (XP, XQ, YP, YM, ZP, ZM, SIB, PAIRO):
        pl.semaphore_signal(barrier, inc=1, device_id=device, device_id_type=MESH)

    @pl.when(not_self)
    def _():
        pl.semaphore_signal(barrier, inc=1, device_id=TDST, device_id_type=MESH)
        pl.semaphore_signal(barrier, inc=1, device_id=TSRC, device_id_type=MESH)

    pl.semaphore_wait(barrier, jnp.where(is_self, 8, 10))

    def own(lo, rows, device):
        return send(g_in.at[0, pl.ds(lo, rows)], shard(0, 0, lo, rows), device)

    gp0, gq0, gzp0, gzm0 = own(0, H0, XP), own(0, H0, XQ), own(0, H0, ZP), own(0, H0, ZM)
    xyp_own, xym_own = send(xcols(k), xslot(0, gs), YP), send(xcols(k), xslot(0, gs), YM)
    xa_sib = send(xcols(SIB[1]), xslot(0, gs), SIB)
    xa_pair = send(xcols(XP[1]), xslot(0, gs), XP)
    gq1, gzp1, gzm1 = own(H0, H1, XQ), own(H0, H1, ZP), own(H0, H1, ZM)

    def both(ref, plus, minus):
        return send(ref, ref, plus), send(ref, ref, minus)

    def to_sibling(dz, lo, rows):
        ref = G.at[m4(z + dz), c, :, pl.ds(lo, rows)]
        return send(ref, ref, SIB)

    def on(ref, device):
        return send(ref, ref, device)

    DZ = (0, -1, 1, 2)
    PB, RS, LO, ROWS = (PB0, PB1), (RS0, RS1), (0, H0), (H0, H1)

    def dx_part(h, r, core, cores=1):
        n = ROWS[h]
        rows = G[m4(z + DZ[r]), pl.ds(core, cores), :, pl.ds(LO[h], n), :].reshape(cores * 4 * n, N)
        part = lax.dot_general(rows, W[...], (((1,), (1,)), ((), ())), preferred_element_type=F32)
        PB[h][r, pl.ds(core * 2, cores * 2)] = part.astype(BF).reshape(cores * 2, 2, n, 512)

    def land(dy):
        return m4(y + dy - k)

    def rs_start(h, r, nr):
        rr, pb, rs = pl.ds(r, nr), PB[h], RS[h]
        return (
            send(pb.at[rr, land(2), 0], rs.at[rr, 0, 0], YP),
            send(pb.at[rr, land(2), 1], rs.at[rr, 1, 0], YM),
            send(pb.at[rr, land(1), 1], rs.at[rr, 0, 1], YP),
            send(pb.at[rr, land(-1), 0], rs.at[rr, 1, 1], YM),
        )

    def rs_mid(h, r, nr, copies):
        rr, pb, rs = pl.ds(r, nr), PB[h], RS[h]
        done = []
        for way, dy, device in ((0, 1, YP), (1, -1, YM)):
            got(copies[way])
            total = rs[rr, way, 0].astype(F32) + pb[rr, land(dy), way].astype(F32)
            rs[rr, way, 0] = total.astype(BF)
            done.append(send(rs.at[rr, way, 0], rs.at[rr, way, 2], device))
        return (copies[2], copies[3], *done)

    last = []

    def rs_end(h, r, nr, copies):
        rr, pb, rs = pl.ds(r, nr), PB[h], RS[h]
        got(*copies)
        for way in range(2):
            total = pb[rr, land(0), way].astype(F32) + rs[rr, 1 - way, 1].astype(F32)
            rs[rr, way, 2] = (total + rs[rr, way, 2].astype(F32)).astype(BF)
            for q in range(r, r + nr):
                row = pl.multiple_of(m4(z + DZ[q]) * 256 + way * 128 + LO[h], 16)
                src, dst = rs.at[q, way, 2], dx_out.at[0, pl.ds(row, ROWS[h])]
                remote = pltpu.make_async_remote_copy(
                    src_ref=src,
                    dst_ref=dst,
                    send_sem=ssem.at[NMSG - 1 - len(last)],
                    recv_sem=rsem.at[NMSG - 1 - len(last)],
                    device_id=TDST,
                    device_id_type=MESH,
                )
                local = pltpu.make_async_copy(src, dst, lsem.at[4 + len(last)])
                last.append((remote, local))
                pl.when(not_self)(remote.start)
                pl.when(is_self)(local.start)

    def dw_block(dz, mode):
        zi = m4(z + dz)

        def tile(i, carry):
            cols = pl.ds(pl.multiple_of(i * TILE, 128), TILE)
            prod = lax.dot_general(
                X[zi].reshape(1024, 512),
                G[zi, :, :, :, cols].reshape(1024, TILE),
                (((0,), (0,)), ((), ())),
                preferred_element_type=F32,
            )
            if mode == 0:
                ACC[:, cols] = prod
            elif mode == 1:
                ACC[:, cols] += prod
            else:
                DWB[:, cols] = (ACC[:, cols] + prod).astype(BF)
            return carry

        tile(0, 0)

    P_, Q_ = to_p, -to_p
    got(xa_sib)
    xyp_sib, xym_sib = both(xslot(0, gs_sib), YP, YM)
    got(gq0)
    gp1 = own(H0, H1, XP)
    zsp1, zsm1 = both(shard(0, Q_, 0, H0), ZP, ZM)
    got(xyp_own, xym_own)
    xfp_own = on(xslot(-1, gs), YP)
    got(xyp_sib, xym_sib)
    xfm_sib = on(xslot(1, gs_sib), YM)

    got(gp0)
    gf0 = on(shard(0, P_, 0, H0), XQ)
    zsp0, zsm0 = both(shard(0, P_, 0, H0), ZP, ZM)
    xa_pairo = send(xcols(PAIRO[1]), xslot(0, gs), PAIRO)
    got(xa_pair)
    xyp_pair, xym_pair = both(xslot(0, gs_pair), YP, YM)
    got(gp1)
    gf1 = on(shard(0, P_, H0, H1), XQ)
    got(gq1, gzp0, gzm0)

    got(gf0)
    own_g.wait()
    sib0a = to_sibling(0, 0, H0)
    zsp2, zsm2 = both(shard(0, 2, 0, H0), ZP, ZM)
    got(gzp1)
    xsp0, xsq0 = both(shard(-1, 0, H0, H1), XP, XQ)
    got(gzm1)
    xsp1, xsq1 = both(shard(1, 0, H0, H1), XP, XQ)
    own_w.wait()
    own_x.wait()
    dx_part(0, 0, c)
    got(xa_pairo)
    xyp_pairo, xym_pairo = both(xslot(0, gs_pairo), YP, YM)
    got(sib0a)
    dx_part(0, 0, oc)
    s0a = rs_start(0, 0, 1)
    got(gf1)
    sib0b = to_sibling(0, H0, H1)
    got(xyp_pair, xym_pair)
    xfp_pair = on(xslot(-1, gs_pair), YP)
    got(zsp0, zsm0, zsp1, zsm1)
    gzp2 = on(shard(-1, 0, 0, H0), ZP)
    gzm2 = on(shard(1, 0, H0, H1), ZM)
    got(sib0b)
    dx_part(1, 0, 0, 2)
    s0b = rs_start(1, 0, 1)
    got(xsp0)
    xt0 = on(shard(-1, P_, H0, H1), XQ)
    got(xym_pairo, xyp_pairo)
    xfm_pairo = on(xslot(1, gs_pairo), YM)
    s0a = rs_mid(0, 0, 1, s0a)
    got(zsp2, zsm2)
    sib1a, sib2a = to_sibling(-1, 0, H0), to_sibling(1, 0, H0)
    ztp0, ztm1 = on(shard(-1, P_, 0, H0), ZP), on(shard(1, Q_, 0, H0), ZM)
    got(xsq1)
    xt1 = on(shard(1, Q_, H0, H1), XP)
    dx_part(0, 1, c)
    dx_part(0, 2, c)
    s0b = rs_mid(1, 0, 1, s0b)
    got(sib1a, sib2a)
    dx_part(0, 1, oc)
    dx_part(0, 2, oc)
    s1a = rs_start(0, 1, 2)
    got(xsq0, xt0)
    sib1b = to_sibling(-1, H0, H1)
    got(xsp1, xt1)
    sib2b = to_sibling(1, H0, H1)
    got(gzm2)
    xsp2, xsq2 = both(shard(2, 0, H0, H1), XP, XQ)
    ztp2, ztm2 = on(shard(-1, 2, 0, H0A), ZP), on(shard(1, 2, H0A, H0 - H0A), ZM)
    rs_end(0, 0, 1, s0a)
    got(sib1b)
    dx_part(1, 1, 0, 2)
    got(sib2b)
    dx_part(1, 2, 0, 2)
    s1b = rs_start(1, 1, 2)
    s1a = rs_mid(0, 1, 2, s1a)
    got(xsp2)
    xt2a = on(shard(2, P_, H0, H1A), XQ)
    got(xsq2)
    xt2b = on(shard(2, Q_, H0 + H1A, H1 - H1A), XP)
    got(xfp_own, xfm_sib, xfp_pair, xfm_pairo)
    dw_block(0, 0)
    got(xt2a, xt2b)
    sib3b = to_sibling(2, H0, H1)
    rs_end(1, 0, 1, s0b)
    s1b = rs_mid(1, 1, 2, s1b)
    got(gzp2, ztp0, ztm1, ztp2, ztm2)
    sib3a = to_sibling(2, 0, H0)
    got(sib3b)
    dx_part(1, 3, 0, 2)
    s2b = rs_start(1, 3, 1)
    dx_part(0, 3, c)
    got(sib3a)
    dx_part(0, 3, oc)
    s2a = rs_start(0, 3, 1)
    dw_block(-1, 1)
    rs_end(0, 1, 2, s1a)
    s2b = rs_mid(1, 3, 1, s2b)
    s2a = rs_mid(0, 3, 1, s2a)
    dw_block(1, 1)
    rs_end(1, 1, 2, s1b)
    rs_end(1, 3, 1, s2b)
    dw_block(2, 2)
    rs_end(0, 3, 1, s2a)

    out = pltpu.make_async_copy(DWB, dw_out, dsem)
    out.start()
    for copy in sends:
        copy.wait_send()
    for remote, local in last:

        @pl.when(not_self)
        def _(remote=remote):
            remote.wait_send()
            remote.wait_recv()

        pl.when(is_self)(local.wait)
    out.wait()


def copy_kernel(a_in, b_in, a_out, b_out, a_buf, b_buf, in_sem, out_sem):
    parts = []
    for i in range(4):
        rows = pl.ds(i * 128, 128)
        parts.append((b_in.at[rows], b_buf.at[rows], b_out.at[rows]))
    for i in range(4):
        rows = pl.ds(i * 256, 256)
        parts.append((a_in.at[0, rows], a_buf.at[rows], a_out.at[0, rows]))
    reads = [pltpu.make_async_copy(p[0], p[1], in_sem.at[i]) for i, p in enumerate(parts)]
    writes = [pltpu.make_async_copy(p[1], p[2], out_sem.at[i]) for i, p in enumerate(parts)]
    for read in reads:
        read.start()
    for read, write in zip(reads, writes):
        read.wait()
        write.start()
    for write in writes:
        write.wait()


def body(layer_input, qkv_grad, qkv_weight):
    anyspec = pl.BlockSpec(memory_space=pl.ANY)
    results = pl.pallas_call(
        kernel,
        out_shape=(
            jax.ShapeDtypeStruct((1, 1024, 512), BF),
            jax.ShapeDtypeStruct((512, N), BF),
        ),
        in_specs=[anyspec] * 3,
        out_specs=(anyspec, anyspec),
        scratch_shapes=[
            pltpu.VMEM((4, 2, 4, 128, N), BF),
            pltpu.VMEM((4, 4, 256, 512), BF),
            pltpu.VMEM((512, N), BF),
            pltpu.VMEM((4, 4, 2, H0, 512), BF),
            pltpu.VMEM((4, 4, 2, H1, 512), BF),
            pltpu.VMEM((4, 2, 3, H0, 512), BF),
            pltpu.VMEM((4, 2, 3, H1, 512), BF),
            pltpu.VMEM((512, N), F32),
            pltpu.VMEM((512, N), BF),
            pltpu.SemaphoreType.DMA((NMSG,)),
            pltpu.SemaphoreType.DMA((NMSG,)),
            pltpu.SemaphoreType.DMA((20,)),
            pltpu.SemaphoreType.DMA,
        ],
        compiler_params=pltpu.CompilerParams(
            collective_id=1, has_side_effects=True, vmem_limit_bytes=60 * 2**20
        ),
        cost_estimate=pl.CostEstimate(
            flops=4 * 4096 * 512 * N, bytes_accessed=8 * 2**20, transcendentals=0
        ),
    )(layer_input, qkv_grad, qkv_weight)
    return pl.pallas_call(
        copy_kernel,
        out_shape=tuple(jax.ShapeDtypeStruct(r.shape, BF) for r in results),
        in_specs=[anyspec] * 2,
        out_specs=(anyspec, anyspec),
        scratch_shapes=[
            pltpu.VMEM((1024, 512), BF),
            pltpu.VMEM((512, N), BF),
            pltpu.SemaphoreType.DMA((8,)),
            pltpu.SemaphoreType.DMA((8,)),
        ],
        compiler_params=pltpu.CompilerParams(vmem_limit_bytes=60 * 2**20),
        cost_estimate=pl.CostEstimate(flops=0, bytes_accessed=7 * 2**20, transcendentals=0),
    )(*results)


def solution(mesh):
    return jax.shard_map(
        body,
        mesh=mesh,
        in_specs=(P("gy", "gz", "gx"), P("gy", "gx", "gz"), P(("gx", "gy"), "gz")),
        out_specs=(P("gy", None, ("gx", "gz")), P(("gx", "gy"), "gz")),
        check_vma=False,
    )
```

```python
import jax
import jax.numpy as jnp
from jax import lax
from jax.experimental import pallas as pl
from jax.experimental.pallas import tpu as pltpu
from jax.sharding import PartitionSpec as P

MESH = pl.DeviceIdType.MESH
BF = jnp.bfloat16
F32 = jnp.float32
N = 2304
NMSG = 128
TILE = 2304
H0, H1 = 80, 48
H0A, H1A = 32, 32


def m4(v):
    return lax.rem(v + 8, 4)


def swap12(v):
    return lax.div(v, 2) + 2 * lax.rem(v, 2)


def kernel(x_in, g_in, w_in, dx_out, dw_out, G, X, W, PB0, PB1, RS0, RS1, ACC, DWB, ssem, rsem, lsem, dsem):
    gx, gy, gz = lax.axis_index("gx"), lax.axis_index("gy"), lax.axis_index("gz")
    x_hi, z = lax.rem(gx, 2), lax.div(gx, 2)
    x_lo, c = lax.div(gy, 2), lax.rem(gy, 2)
    x, y, k = x_hi * 2 + x_lo, gz, gy
    oc = 1 - c

    def dev(dx=0, dy=0, dz=0):
        xx = m4(x + dx)
        return (m4(z + dz) * 2 + lax.div(xx, 2), lax.rem(xx, 2) * 2 + c, m4(y + dy))

    to_p = 1 - 2 * x_lo
    XP, XQ = dev(dx=to_p), dev(dx=-to_p)
    YP, YM, ZP, ZM = dev(dy=1), dev(dy=-1), dev(dz=1), dev(dz=-1)
    SIB = (gx, x_lo * 2 + oc, y)
    PAIRO = (gx, (1 - x_lo) * 2 + oc, y)
    is_self = jnp.logical_and(k == 0, y == 0)
    not_self = jnp.logical_not(is_self)
    TDST = (gx, swap12(m4(y - k)), k)
    TSRC = (gx, y, m4(y + swap12(k)))

    sends = []

    def send(src, dst, device):
        i = len(sends)
        copy = pltpu.make_async_remote_copy(
            src_ref=src,
            dst_ref=dst,
            send_sem=ssem.at[i],
            recv_sem=rsem.at[i],
            device_id=device,
            device_id_type=MESH,
        )
        sends.append(copy)
        copy.start()
        return copy

    def got(*copies):
        for copy in copies:
            copy.wait_recv()

    def shard(dz, dx, lo=0, rows=128, core=None):
        xx = m4(x + dx)
        slot = lax.rem(xx, 2) * 2 + lax.div(xx, 2)
        return G.at[m4(z + dz), c if core is None else core, slot, pl.ds(lo, rows)]

    def xcols(kk):
        return x_in.at[0, :, pl.ds(pl.multiple_of(kk * 512, 512), 512)]

    gs, gs_sib, gs_pair, gs_pairo = c * 2 + x_lo, oc * 2 + x_lo, c * 2 + 1 - x_lo, oc * 2 + 1 - x_lo

    def xslot(dy, g):
        return X.at[m4(y + dy), g]

    own_g = pltpu.make_async_copy(g_in.at[0], shard(0, 0), lsem.at[0])
    own_g.start()
    own_x = pltpu.make_async_copy(xcols(k), xslot(0, gs), lsem.at[1])
    own_x.start()
    own_w = pltpu.make_async_copy(w_in, W, lsem.at[2])
    own_w.start()

    barrier = pltpu.get_barrier_semaphore()
    for device in (XP, XQ, YP, YM, ZP, ZM, SIB, PAIRO):
        pl.semaphore_signal(barrier, inc=1, device_id=device, device_id_type=MESH)

    @pl.when(not_self)
    def _():
        pl.semaphore_signal(barrier, inc=1, device_id=TDST, device_id_type=MESH)
        pl.semaphore_signal(barrier, inc=1, device_id=TSRC, device_id_type=MESH)

    pl.semaphore_wait(barrier, jnp.where(is_self, 8, 10))

    def own(lo, rows, device):
        return send(g_in.at[0, pl.ds(lo, rows)], shard(0, 0, lo, rows), device)

    gp0, gq0, gzp0, gzm0 = own(0, H0, XP), own(0, H0, XQ), own(0, H0, ZP), own(0, H0, ZM)
    xyp_own, xym_own = send(xcols(k), xslot(0, gs), YP), send(xcols(k), xslot(0, gs), YM)
    xa_sib = send(xcols(SIB[1]), xslot(0, gs), SIB)
    xa_pair = send(xcols(XP[1]), xslot(0, gs), XP)
    gq1, gzp1, gzm1 = own(H0, H1, XQ), own(H0, H1, ZP), own(H0, H1, ZM)

    def both(ref, plus, minus):
        return send(ref, ref, plus), send(ref, ref, minus)

    def to_sibling(dz, lo, rows):
        ref = G.at[m4(z + dz), c, :, pl.ds(lo, rows)]
        return send(ref, ref, SIB)

    def on(ref, device):
        return send(ref, ref, device)

    DZ = (0, -1, 1, 2)
    PB, RS, LO, ROWS = (PB0, PB1), (RS0, RS1), (0, H0), (H0, H1)

    def dx_part(h, r, core, cores=1):
        n = ROWS[h]
        rows = G[m4(z + DZ[r]), pl.ds(core, cores), :, pl.ds(LO[h], n), :].reshape(cores * 4 * n, N)
        part = lax.dot_general(rows, W[...], (((1,), (1,)), ((), ())), preferred_element_type=F32)
        PB[h][r, pl.ds(core * 2, cores * 2)] = part.astype(BF).reshape(cores * 2, 2, n, 512)

    def land(dy):
        return m4(y + dy - k)

    def rs_start(h, r, nr):
        rr, pb, rs = pl.ds(r, nr), PB[h], RS[h]
        return (
            send(pb.at[rr, land(2), 0], rs.at[rr, 0, 0], YP),
            send(pb.at[rr, land(2), 1], rs.at[rr, 1, 0], YM),
            send(pb.at[rr, land(1), 1], rs.at[rr, 0, 1], YP),
            send(pb.at[rr, land(-1), 0], rs.at[rr, 1, 1], YM),
        )

    def rs_mid(h, r, nr, copies):
        rr, pb, rs = pl.ds(r, nr), PB[h], RS[h]
        done = []
        for way, dy, device in ((0, 1, YP), (1, -1, YM)):
            got(copies[way])
            total = rs[rr, way, 0].astype(F32) + pb[rr, land(dy), way].astype(F32)
            rs[rr, way, 0] = total.astype(BF)
            done.append(send(rs.at[rr, way, 0], rs.at[rr, way, 2], device))
        return (copies[2], copies[3], *done)

    last = []

    def rs_end(h, r, nr, copies):
        rr, pb, rs = pl.ds(r, nr), PB[h], RS[h]
        got(*copies)
        for way in range(2):
            total = pb[rr, land(0), way].astype(F32) + rs[rr, 1 - way, 1].astype(F32)
            rs[rr, way, 2] = (total + rs[rr, way, 2].astype(F32)).astype(BF)
            for q in range(r, r + nr):
                row = pl.multiple_of(m4(z + DZ[q]) * 256 + way * 128 + LO[h], 16)
                src, dst = rs.at[q, way, 2], dx_out.at[0, pl.ds(row, ROWS[h])]
                remote = pltpu.make_async_remote_copy(
                    src_ref=src,
                    dst_ref=dst,
                    send_sem=ssem.at[NMSG - 1 - len(last)],
                    recv_sem=rsem.at[NMSG - 1 - len(last)],
                    device_id=TDST,
                    device_id_type=MESH,
                )
                local = pltpu.make_async_copy(src, dst, lsem.at[4 + len(last)])
                last.append((remote, local))
                pl.when(not_self)(remote.start)
                pl.when(is_self)(local.start)

    def dw_block(dz, mode):
        zi = m4(z + dz)

        def tile(i, carry):
            cols = pl.ds(pl.multiple_of(i * TILE, 128), TILE)
            prod = lax.dot_general(
                X[zi].reshape(1024, 512),
                G[zi, :, :, :, cols].reshape(1024, TILE),
                (((0,), (0,)), ((), ())),
                preferred_element_type=F32,
            )
            if mode == 0:
                ACC[:, cols] = prod
            elif mode == 1:
                ACC[:, cols] += prod
            else:
                DWB[:, cols] = (ACC[:, cols] + prod).astype(BF)
            return carry

        tile(0, 0)

    P_, Q_ = to_p, -to_p
    got(xa_sib)
    xyp_sib, xym_sib = both(xslot(0, gs_sib), YP, YM)
    got(gq0)
    gp1 = own(H0, H1, XP)
    zsp1, zsm1 = both(shard(0, Q_, 0, H0), ZP, ZM)
    got(xyp_own, xym_own)
    xfp_own = on(xslot(-1, gs), YP)
    got(xyp_sib, xym_sib)
    xfm_sib = on(xslot(1, gs_sib), YM)

    got(gp0)
    gf0 = on(shard(0, P_, 0, H0), XQ)
    zsp0, zsm0 = both(shard(0, P_, 0, H0), ZP, ZM)
    xa_pairo = send(xcols(PAIRO[1]), xslot(0, gs), PAIRO)
    got(xa_pair)
    xyp_pair, xym_pair = both(xslot(0, gs_pair), YP, YM)
    got(gp1)
    gf1 = on(shard(0, P_, H0, H1), XQ)
    got(gq1, gzp0, gzm0)

    got(gf0)
    own_g.wait()
    sib0a = to_sibling(0, 0, H0)
    zsp2, zsm2 = both(shard(0, 2, 0, H0), ZP, ZM)
    got(gzp1)
    xsp0, xsq0 = both(shard(-1, 0, H0, H1), XP, XQ)
    got(gzm1)
    xsp1, xsq1 = both(shard(1, 0, H0, H1), XP, XQ)
    own_w.wait()
    own_x.wait()
    dx_part(0, 0, c)
    got(xa_pairo)
    xyp_pairo, xym_pairo = both(xslot(0, gs_pairo), YP, YM)
    got(sib0a)
    dx_part(0, 0, oc)
    s0a = rs_start(0, 0, 1)
    got(gf1)
    sib0b = to_sibling(0, H0, H1)
    got(xyp_pair, xym_pair)
    xfp_pair = on(xslot(-1, gs_pair), YP)
    got(zsp0, zsm0, zsp1, zsm1)
    gzp2 = on(shard(-1, 0, 0, H0), ZP)
    gzm2 = on(shard(1, 0, H0, H1), ZM)
    got(sib0b)
    dx_part(1, 0, 0, 2)
    s0b = rs_start(1, 0, 1)
    got(xsp0)
    xt0 = on(shard(-1, P_, H0, H1), XQ)
    got(xym_pairo, xyp_pairo)
    xfm_pairo = on(xslot(1, gs_pairo), YM)
    s0a = rs_mid(0, 0, 1, s0a)
    got(zsp2, zsm2)
    sib1a, sib2a = to_sibling(-1, 0, H0), to_sibling(1, 0, H0)
    ztp0, ztm1 = on(shard(-1, P_, 0, H0), ZP), on(shard(1, Q_, 0, H0), ZM)
    got(xsq1)
    xt1 = on(shard(1, Q_, H0, H1), XP)
    dx_part(0, 1, c)
    dx_part(0, 2, c)
    s0b = rs_mid(1, 0, 1, s0b)
    got(sib1a, sib2a)
    dx_part(0, 1, oc)
    dx_part(0, 2, oc)
    s1a = rs_start(0, 1, 2)
    got(xsq0, xt0)
    sib1b = to_sibling(-1, H0, H1)
    got(xsp1, xt1)
    sib2b = to_sibling(1, H0, H1)
    got(gzm2)
    xsp2, xsq2 = both(shard(2, 0, H0, H1), XP, XQ)
    ztp2, ztm2 = on(shard(-1, 2, 0, H0A), ZP), on(shard(1, 2, H0A, H0 - H0A), ZM)
    rs_end(0, 0, 1, s0a)
    got(sib1b)
    dx_part(1, 1, 0, 2)
    got(sib2b)
    dx_part(1, 2, 0, 2)
    s1b = rs_start(1, 1, 2)
    s1a = rs_mid(0, 1, 2, s1a)
    got(xsp2)
    xt2a = on(shard(2, P_, H0, H1A), XQ)
    got(xsq2)
    xt2b = on(shard(2, Q_, H0 + H1A, H1 - H1A), XP)
    got(xfp_own, xfm_sib, xfp_pair, xfm_pairo)
    dw_block(0, 0)
    got(xt2a, xt2b)
    sib3b = to_sibling(2, H0, H1)
    rs_end(1, 0, 1, s0b)
    s1b = rs_mid(1, 1, 2, s1b)
    got(gzp2, ztp0, ztm1, ztp2, ztm2)
    sib3a = to_sibling(2, 0, H0)
    got(sib3b)
    dx_part(1, 3, 0, 2)
    s2b = rs_start(1, 3, 1)
    dx_part(0, 3, c)
    got(sib3a)
    dx_part(0, 3, oc)
    s2a = rs_start(0, 3, 1)
    dw_block(-1, 1)
    rs_end(0, 1, 2, s1a)
    s2b = rs_mid(1, 3, 1, s2b)
    s2a = rs_mid(0, 3, 1, s2a)
    dw_block(1, 1)
    rs_end(1, 1, 2, s1b)
    rs_end(1, 3, 1, s2b)
    dw_block(2, 2)
    out = pltpu.make_async_copy(DWB, dw_out, dsem)
    out.start()
    rs_end(0, 3, 1, s2a)

    for copy in sends:
        copy.wait_send()
    for remote, local in last:

        @pl.when(not_self)
        def _(remote=remote):
            remote.wait_send()
            remote.wait_recv()

        pl.when(is_self)(local.wait)
    out.wait()


def copy_kernel(a_in, b_in, a_out, b_out, a_buf, b_buf, in_sem, out_sem):
    parts = []
    for i in range(8):
        rows = pl.ds(i * 64, 64)
        parts.append((b_in.at[rows], b_buf.at[rows], b_out.at[rows]))
    for i in range(4):
        rows = pl.ds(i * 256, 256)
        parts.append((a_in.at[0, rows], a_buf.at[rows], a_out.at[0, rows]))
    reads = [pltpu.make_async_copy(p[0], p[1], in_sem.at[i]) for i, p in enumerate(parts)]
    writes = [pltpu.make_async_copy(p[1], p[2], out_sem.at[i]) for i, p in enumerate(parts)]
    for read in reads:
        read.start()
    for read, write in zip(reads, writes):
        read.wait()
        write.start()
    for write in writes:
        write.wait()


def body(layer_input, qkv_grad, qkv_weight):
    anyspec = pl.BlockSpec(memory_space=pl.ANY)
    results = pl.pallas_call(
        kernel,
        out_shape=(
            jax.ShapeDtypeStruct((1, 1024, 512), BF),
            jax.ShapeDtypeStruct((512, N), BF),
        ),
        in_specs=[anyspec] * 3,
        out_specs=(anyspec, anyspec),
        scratch_shapes=[
            pltpu.VMEM((4, 2, 4, 128, N), BF),
            pltpu.VMEM((4, 4, 256, 512), BF),
            pltpu.VMEM((512, N), BF),
            pltpu.VMEM((4, 4, 2, H0, 512), BF),
            pltpu.VMEM((4, 4, 2, H1, 512), BF),
            pltpu.VMEM((4, 2, 3, H0, 512), BF),
            pltpu.VMEM((4, 2, 3, H1, 512), BF),
            pltpu.VMEM((512, N), F32),
            pltpu.VMEM((512, N), BF),
            pltpu.SemaphoreType.DMA((NMSG,)),
            pltpu.SemaphoreType.DMA((NMSG,)),
            pltpu.SemaphoreType.DMA((20,)),
            pltpu.SemaphoreType.DMA,
        ],
        compiler_params=pltpu.CompilerParams(
            collective_id=1, has_side_effects=True, vmem_limit_bytes=60 * 2**20
        ),
        cost_estimate=pl.CostEstimate(
            flops=4 * 4096 * 512 * N, bytes_accessed=8 * 2**20, transcendentals=0
        ),
    )(layer_input, qkv_grad, qkv_weight)
    return pl.pallas_call(
        copy_kernel,
        out_shape=tuple(jax.ShapeDtypeStruct(r.shape, BF) for r in results),
        in_specs=[anyspec] * 2,
        out_specs=(anyspec, anyspec),
        scratch_shapes=[
            pltpu.VMEM((1024, 512), BF),
            pltpu.VMEM((512, N), BF),
            pltpu.SemaphoreType.DMA((12,)),
            pltpu.SemaphoreType.DMA((12,)),
        ],
        compiler_params=pltpu.CompilerParams(vmem_limit_bytes=60 * 2**20),
        cost_estimate=pl.CostEstimate(flops=0, bytes_accessed=7 * 2**20, transcendentals=0),
    )(*results)


def solution(mesh):
    return jax.shard_map(
        body,
        mesh=mesh,
        in_specs=(P("gy", "gz", "gx"), P("gy", "gx", "gz"), P(("gx", "gy"), "gz")),
        out_specs=(P("gy", None, ("gx", "gz")), P(("gx", "gy"), "gz")),
        check_vma=False,
    )
```
